32 devices in a mesh: scalp: 16 (over z, y, x), screen: 2 (over core).
Axes of the slice: x: 2, y: 2, z: 4, core: 2. Of those that a mesh axis runs over, the one named last changes fastest.
Arguments:
- guides: bfloat16 [65536, 384], P('scalp'), may hold values from -6 to 6
- neighbours: int32 [128, 32], P(('scalp', 'screen')), may hold values from 0 to 65535, as said below
- pick: int32 [128, 4, 256], P(('scalp', 'screen')), may hold values from 0 to 31, as said below
- pick_weight: bfloat16 [128, 4, 256], P(('scalp', 'screen')), may hold values from 0.099609375 to 0.59765625
- keep: int32 [128, 256], P(('scalp', 'screen')), may hold values 0 or 1
- width: float32 [128, 256], P(('scalp', 'screen')), may hold values from 0.2 to 2
- route: int32 [128, 1], P(('scalp', 'screen')), may hold values from 0 to 1; in each aligned block of 4 rows (0 to 3, 4 to 7, ...) at most 3 rows name the same one
- tess_centre: bfloat16 [2, 384, 768], P('screen'), may hold values from -0.3125 to 0.3125
- tess_side: bfloat16 [2, 384, 768], P('screen'), may hold values from -0.3125 to 0.3125
Outputs:
- ribbon: bfloat16 [49152, 768], P(('scalp', 'screen'))
The draws below stay inside these ranges and needn't reach their ends.
Inputs may be any that keep to these rules, and one draw needn't show every extreme that they name: `neighbours`: each entry names a guide of the render block's own scalp tile or of the scalp tile just before or after it, wrapping around; a block of device (s, c) belongs to scalp tile s. `pick`: the 4 entries of one render strand differ. `route`: among the 4 blocks of one device at most 3 name the same screen tile.
All inputs are finite; a program needn't handle non-finite values. No bound on the sum of `keep` on one device may be relied on, other than what follows from the above.
Results may differ from the reference program's by a relative error of at most 0.009.
Values may be sent and summed in bfloat16 or wider, within the bound.
A program may use at most 64 MiB of HBM per device.

```python
import math
import jax
import jax.numpy as jnp
import numpy as np
from jax import lax

P_SIZE = 128
BLK = 256
K = 32
J = 4
RB = 4
GT = 4096
TILES = 16
SCREENS = 2
CAP = 3
GUIDES = 65536
RBLOCKS = 128


def draw_neighbours(key, part):
    first, second = jax.random.split(key)
    block = jnp.arange(RBLOCKS, dtype=jnp.int32)
    home = block // (RB * SCREENS)
    offset = jax.random.randint(first, (RBLOCKS, K), -1, 2).astype(jnp.int32)
    within = jax.random.randint(second, (RBLOCKS, K), 0, GT).astype(jnp.int32)
    offset = offset.at[0, 0].set(0).at[RBLOCKS - 1, K - 1].set(0)
    within = within.at[0, 0].set(0).at[RBLOCKS - 1, K - 1].set(GT - 1)
    return ((home[:, None] + offset) % TILES * GT + within).astype(jnp.int32)


def draw_pick(key, part):
    scores = jax.random.randint(key, (RBLOCKS, BLK, K), 0, 1 << 20).astype(jnp.int32) * K + jnp.arange(K, dtype=jnp.int32)
    order = jnp.argsort(scores, axis=-1)[..., :J]
    return jnp.transpose(order, (0, 2, 1)).astype(jnp.int32)


def set_ends(drawn, key, least, high):
    index_at = [jax.random.randint(jax.random.fold_in(key, axis), (), 0, length) for axis, length in enumerate(drawn.shape)]
    widest = drawn.shape.index(max(drawn.shape))
    beside = index_at[:widest] + [(index_at[widest] + 1) % drawn.shape[widest]] + index_at[widest + 1:]
    return drawn.at[tuple(index_at)].set(least).at[tuple(beside)].set(high)


def block_scale(own_key, extent, shards, low, largest):
    loudness, own = 1.0, jax.random.fold_in(own_key, 6)
    for dim, blocks in shards:
        heights = jnp.exp(jax.random.uniform(jax.random.fold_in(own, dim), (blocks,), jnp.float32, low / len(shards), largest / len(shards)))
        loudness = loudness * jnp.repeat(heights, extent[dim] // blocks).reshape([-1 if axis == dim else 1 for axis in range(len(extent))])
    return loudness


def shared_out(rng, own, number, rows, amount, top, most, slope):
    ranking = jax.random.permutation(rng, amount)
    heavy_load, usual = shares(amount, rows * top, most, slope, True), shares(amount, rows * top, most, slope, False)
    places = jnp.arange(amount)

    def named(tallies, turn):
        used = int((tallies > 0).sum())
        fixed = max(1, used // 4)
        passed = fixed + (places - fixed + turn * (used - fixed)) % max(1, amount - fixed)
        return jnp.zeros((amount,), jnp.int32).at[ranking[jnp.where(places < fixed, places, passed)]].set(jnp.asarray(tallies, jnp.int32))

    tallies = jnp.where(number % 4 == 0, named(heavy_load, number // 4), named(usual, number - number // 4 - 1))
    mixed = jax.random.permutation(jax.random.fold_in(own, 3), amount)
    source_of, taker = mixed[0:amount // 2 * 2:2], mixed[1:amount // 2 * 2:2]
    margin = jnp.minimum(tallies[source_of] - 1, most - tallies[taker]) // 2
    margin = jnp.where((source_of == ranking[0]) | (taker == ranking[0]) | (tallies[taker] == 0), 0, jnp.maximum(margin, 0))
    passed = jax.random.randint(jax.random.fold_in(own, 4), (amount // 2,), 0, 1 << 20) % (margin + 1)
    tallies = tallies.at[source_of].add(-passed).at[taker].add(passed)
    members = jnp.searchsorted(jnp.cumsum(tallies), jnp.arange(rows * top), side="right").astype(jnp.int32)
    table = members.reshape(top, rows).T
    table = table[jax.random.permutation(jax.random.fold_in(own, 1), rows)]
    turn = jax.random.randint(jax.random.fold_in(own, 2), (rows, 1), 0, top)
    return jnp.take_along_axis(table, (jnp.arange(top)[None, :] + turn) % top, axis=1)


def shares(count, total, reach, lean, full):
    weights = [(1 << 20) // math.isqrt(rank ** lean) + 1 for rank in range(1, count + 1)]
    largest = reach if full else min(reach, max(-(-total // count), total * weights[0] // sum(weights)))
    least = 1 if total - largest >= count - 1 else 0
    holding, rest = [largest] + [least] * (count - 1), total - largest - least * (count - 1)
    while rest > 0:
        free = [i for i in range(1, count) if holding[i] < largest] or [i for i in range(1, count) if holding[i] < reach]
        pool, left = sum([weights[i] for i in free]), rest
        for i in free:
            addition = min(reach - holding[i], max(1, left * weights[i] // pool), rest)
            holding[i] = holding[i] + addition
            rest = rest - addition
    return np.array(holding)


def centred(rng, extent, spread, reach, cuts=(), held_as=jnp.bfloat16):
    result = spread * jax.random.normal(rng, extent, jnp.float32)
    if cuts:
        result = result * block_scale(rng, extent, cuts, -0.22, 0.18)
    return jnp.clip(result, -reach, reach).astype(held_as)


def setup_inputs(seed: int = 0) -> dict:
    splits = jax.random.split(jax.random.key(seed), 10)
    guides = centred(splits[0], (GUIDES, 3 * P_SIZE), 1.0, 6.0, ((0, 16),))
    neighbours = draw_neighbours(jax.random.fold_in(splits[9], 71), 0)
    pick = draw_pick(jax.random.fold_in(splits[9], 71), 0)
    pick_weight = jnp.clip(0.099609375 + 0.49804688 * jax.random.uniform(splits[3], (RBLOCKS, J, BLK), jnp.float32) ** block_scale(splits[3], (RBLOCKS, J, BLK), ((0, 32),), -0.2, 0.2), 0.099609375, 0.59765625).astype(jnp.bfloat16)
    keep = set_ends((jax.random.randint(splits[4], (RBLOCKS, BLK), 0, 4) < 3).astype(jnp.int32), jax.random.fold_in(splits[4], 1), 0, 1)
    width = jnp.clip(jnp.exp(math.log(2.0) - 2.3025851 * jax.random.uniform(splits[5], (RBLOCKS, BLK), jnp.float32) ** block_scale(splits[5], (RBLOCKS, BLK), ((0, 32),), -0.2, 0.2)), 0.2, 2.0)
    route_keys = jax.random.split(jax.random.fold_in(splits[6], 1), RBLOCKS // RB)
    route_turns = jax.random.permutation(jax.random.fold_in(splits[6], 3), RBLOCKS // RB)
    route = jax.vmap(lambda own, number: shared_out(jax.random.fold_in(splits[6], 2), own, number, RB, SCREENS, 1, CAP, 2))(route_keys, route_turns).reshape((RBLOCKS, 1))
    tess_centre = centred(splits[7], (SCREENS, 3 * P_SIZE, 6 * P_SIZE), (3 * P_SIZE) ** -0.5, 0.3125, ((0, 2),))
    tess_side = centred(splits[8], (SCREENS, 3 * P_SIZE, 6 * P_SIZE), (3 * P_SIZE) ** -0.5, 0.3125, ((0, 2),))
    return {"guides": guides, "neighbours": neighbours, "pick": pick, "pick_weight": pick_weight, "keep": keep, "width": width, "route": route, "tess_centre": tess_centre, "tess_side": tess_side}


def blend(picks, weights):
    hit = (picks[..., None] == jnp.arange(K, dtype=jnp.int32)).astype(jnp.float32)
    return jnp.sum(hit * weights.astype(jnp.float32)[..., None], axis=1).astype(jnp.bfloat16)


def reference(guides, neighbours, pick, pick_weight, keep, width, route, tess_centre, tess_side):
    ndev = TILES * SCREENS
    cap = RB // SCREENS + RB // 4

    def one_device(device):
        start = (device * RB).astype(jnp.int32)
        near = lax.dynamic_slice_in_dim(neighbours, start, RB, 0)
        picks = lax.dynamic_slice_in_dim(pick, start, RB, 0)
        weights = lax.dynamic_slice_in_dim(pick_weight, start, RB, 0)
        kept = lax.dynamic_slice_in_dim(keep, start, RB, 0).astype(jnp.float32)
        widths = lax.dynamic_slice_in_dim(width, start, RB, 0)
        tiles = lax.dynamic_slice_in_dim(route, start, RB, 0)[:, 0]
        gathered = guides[near]
        mixing = blend(picks, weights)
        panel = jnp.einsum("rbk,rkx->rbx", mixing.astype(jnp.float32), gathered.astype(jnp.float32)).astype(jnp.bfloat16)
        scaled = widths * BLK / (jnp.sum(kept, axis=1, keepdims=True) + 1.0)
        centre = jnp.einsum("rbx,rxy->rby", panel.astype(jnp.float32), tess_centre[tiles].astype(jnp.float32))
        side = jnp.einsum("rbx,rxy->rby", panel.astype(jnp.float32), tess_side[tiles].astype(jnp.float32))
        return (kept[..., None] * (centre + scaled[..., None] * side)).astype(jnp.bfloat16)

    ribbons = lax.map(one_device, jnp.arange(ndev, dtype=jnp.int32))
    tiles_all = route[:, 0].reshape(ndev, RB)
    same = tiles_all[:, :, None] == tiles_all[:, None, :]
    earlier = jnp.arange(RB)[None, :] < jnp.arange(RB)[:, None]
    rank = jnp.sum(same & earlier[None], axis=2).astype(jnp.int32)
    device = jnp.arange(ndev, dtype=jnp.int32)[:, None]
    scalp_of = device // SCREENS
    screen_of = device % SCREENS
    slot = ((scalp_of * SCREENS + tiles_all) * SCREENS + screen_of) * cap + rank
    placed = jnp.zeros((ndev * SCREENS * cap, BLK, 6 * P_SIZE), jnp.bfloat16)
    placed = placed.at[slot.reshape(-1)].set(ribbons.reshape(ndev * RB, BLK, 6 * P_SIZE))
    return placed.reshape(-1, 6 * P_SIZE)
```

```python
import functools

import jax
import jax.numpy as jnp
from jax import lax
from jax.experimental import pallas as pl
from jax.experimental.pallas import tpu as pltpu
from jax.sharding import PartitionSpec as P

MESH = pl.DeviceIdType.MESH
CHUNK = 512


def columns(lists, lanes):
    parts = []
    for b in range(lists.shape[0]):
        row = jnp.broadcast_to(lists[b : b + 1, :], (lanes, lists.shape[1]))
        parts.append(row.T)
    return jnp.concatenate(parts, axis=0)


def pick_rows(wanted, guides, total):
    rows, lanes = wanted.shape
    tile = guides.shape[0]
    chunk = min(CHUNK, tile)
    lane = lax.broadcasted_iota(jnp.int32, (rows, lanes), 1)
    total[:rows] = jnp.zeros((rows, guides.shape[1]), jnp.float32)

    def body(i, carry):
        base = pl.multiple_of(i * chunk, chunk)
        hit = jnp.concatenate(
            [
                jnp.where(wanted == lane + (base + at), 1.0, 0.0).astype(jnp.bfloat16)
                for at in range(0, chunk, lanes)
            ],
            axis=1,
        )
        total[:rows] += jnp.dot(
            hit, guides[pl.ds(base, chunk), :], preferred_element_type=jnp.float32
        )
        return carry

    lax.fori_loop(0, tile // chunk, body, 0)
    return total[:rows]


def exchange(
    scalps,
    guides_ref,
    near_ref,
    pick_ref,
    weight_ref,
    keep_ref,
    width_ref,
    route_ref,
    rows_ref,
    data_ref,
    tiles_ref,
    guides,
    lists,
    outgoing,
    incoming,
    total,
    local_sem,
    send_sem,
    recv_sem,
):
    here = lax.axis_index("scalp")
    core = lax.axis_index("screen")
    lower = (lax.rem(here + scalps - 1, scalps), core)
    upper = (lax.rem(here + 1, scalps), core)
    pair = (here, 1 - core)
    tile = guides.shape[0]
    blocks, listed = near_ref.shape
    count = blocks * listed
    lanes = 128

    load = pltpu.make_async_copy(guides_ref, guides, local_sem)
    load.start()
    barrier = pltpu.get_barrier_semaphore()
    for other in (lower, upper, pair):
        pl.semaphore_signal(barrier, inc=1, device_id=other, device_id_type=MESH)

    def remote(src, dst, at, to):
        return pltpu.make_async_remote_copy(
            src_ref=src,
            dst_ref=dst,
            send_sem=send_sem.at[at],
            recv_sem=recv_sem.at[at],
            device_id=to,
            device_id_type=MESH,
        )

    kept = keep_ref[...].astype(jnp.float32)
    strands = kept.shape[1]
    scaled = width_ref[...] * strands / (jnp.sum(kept, axis=1, keepdims=True) + 1.0)
    joins = pick_ref.shape[1]
    spare = data_ref.shape[2] - 2 * joins - 2
    for b in range(blocks):
        data_ref[core, b] = jnp.concatenate(
            [
                pick_ref[b].astype(jnp.float32),
                weight_ref[b].astype(jnp.float32),
                kept[b : b + 1],
                (kept * scaled)[b : b + 1],
                jnp.zeros((spare, strands), jnp.float32),
            ],
            axis=0,
        )
    tiles_ref[core] = route_ref[...]
    pl.semaphore_wait(barrier, 3)

    ask_upper = remote(near_ref, lists.at[0], 0, upper)
    ask_lower = remote(near_ref, lists.at[1], 1, lower)
    ask_upper.start()
    ask_lower.start()
    give_data = remote(data_ref.at[core], data_ref.at[core], 2, pair)
    give_data.start()
    give_tiles = remote(tiles_ref.at[core], tiles_ref.at[core], 3, pair)
    give_tiles.start()

    load.wait()
    offset = here * tile
    own = pick_rows(columns(near_ref[...], lanes) - offset, guides, total).astype(jnp.bfloat16)
    rows_ref[core] = own
    ask_upper.wait()
    ask_lower.wait()
    wanted = jnp.concatenate([columns(lists[0], lanes), columns(lists[1], lanes)], axis=0)
    both = pick_rows(wanted - offset, guides, total).astype(jnp.bfloat16)
    outgoing[0] = both[:count]
    outgoing[1] = both[count:]
    to_lower = remote(outgoing.at[0], incoming.at[1], 4, lower)
    to_upper = remote(outgoing.at[1], incoming.at[0], 5, upper)
    to_lower.start()
    to_upper.start()
    to_lower.wait()
    to_upper.wait()
    rows_ref[core] = rows_ref[core] + incoming[0] + incoming[1]
    give_rows = remote(rows_ref.at[core], rows_ref.at[core], 6, pair)
    give_rows.start()
    give_data.wait()
    give_tiles.wait()
    give_rows.wait()


def tessellate(joins, cap, tiles_ref, rows_ref, data_ref, centre_ref, side_ref, out_ref, maps):
    screens, blocks = tiles_ref.shape[:2]
    listed = rows_ref.shape[1] // blocks
    step = pl.program_id(0)

    @pl.when(step == 0)
    def _():
        for c in range(screens):
            for half, table in enumerate((centre_ref, side_ref)):
                made = jnp.dot(
                    rows_ref[c], table[0], preferred_element_type=jnp.float32
                ).astype(jnp.bfloat16)
                for b in range(blocks):
                    maps[c * blocks + b, half * listed : (half + 1) * listed] = made[
                        b * listed : (b + 1) * listed
                    ]

    mine = lax.axis_index("screen")
    source = step // cap
    place = step % cap
    rank = jnp.int32(0)
    block = jnp.int32(0)
    found = jnp.int32(0)
    for b in range(blocks):
        same = (tiles_ref[source, b, 0] == mine).astype(jnp.int32)
        hit = same * (rank == place).astype(jnp.int32)
        block = block + hit * b
        found = found + hit
        rank = rank + same
    data = data_ref[source, block]
    strands = data.shape[1]
    names = lax.broadcasted_iota(jnp.int32, (listed, strands), 0).astype(jnp.float32)
    mix = jnp.zeros((listed, strands), jnp.float32)
    for j in range(joins):
        mix = jnp.where(names == data[j : j + 1], data[joins + j : joins + j + 1], mix)
    mix = mix * found.astype(jnp.float32)
    spread = jnp.concatenate(
        [mix * data[2 * joins : 2 * joins + 1], mix * data[2 * joins + 1 : 2 * joins + 2]], axis=0
    ).astype(jnp.bfloat16)
    out_ref[...] = lax.dot_general(
        spread,
        maps[source * blocks + block],
        (((0,), (0,)), ((), ())),
        preferred_element_type=jnp.float32,
    ).astype(out_ref.dtype)


def shards(guides, neighbours, pick, pick_weight, keep, width, route, tess_centre, tess_side):
    scalps = lax.axis_size("scalp")
    screens = lax.axis_size("screen")
    tile, points = guides.shape
    blocks, listed = neighbours.shape
    strands = keep.shape[1]
    joins = pick.shape[1]
    cap = blocks // screens + blocks // 4
    count = blocks * listed
    fields = -(-(2 * joins + 2) // 8) * 8
    verts = tess_centre.shape[2]
    vmem = pl.BlockSpec(memory_space=pltpu.VMEM)
    rows, data, tiles = pl.pallas_call(
        functools.partial(exchange, scalps),
        out_shape=(
            jax.ShapeDtypeStruct((screens, count, points), jnp.bfloat16),
            jax.ShapeDtypeStruct((screens, blocks, fields, strands), jnp.float32),
            jax.ShapeDtypeStruct((screens, blocks, 1), jnp.int32),
        ),
        in_specs=[pl.BlockSpec(memory_space=pl.ANY)] + [vmem] * 6,
        out_specs=(vmem, vmem, vmem),
        scratch_shapes=[
            pltpu.VMEM((tile, points), jnp.bfloat16),
            pltpu.VMEM((2, blocks, listed), jnp.int32),
            pltpu.VMEM((2, count, points), jnp.bfloat16),
            pltpu.VMEM((2, count, points), jnp.bfloat16),
            pltpu.VMEM((2 * count, points), jnp.float32),
            pltpu.SemaphoreType.DMA,
            pltpu.SemaphoreType.DMA((7,)),
            pltpu.SemaphoreType.DMA((7,)),
        ],
        compiler_params=pltpu.CompilerParams(
            collective_id=0, has_side_effects=True, vmem_limit_bytes=24 * 1024 * 1024
        ),
    )(guides, neighbours, pick, pick_weight, keep, width, route)
    whole = lambda a: pl.BlockSpec(a.shape, lambda i: (0,) * a.ndim)
    return pl.pallas_call(
        functools.partial(tessellate, joins, cap),
        grid=(screens * cap,),
        out_shape=jax.ShapeDtypeStruct((screens * cap * strands, verts), jnp.bfloat16),
        in_specs=[
            pl.BlockSpec(memory_space=pltpu.SMEM),
            whole(rows),
            whole(data),
            whole(tess_centre),
            whole(tess_side),
        ],
        out_specs=pl.BlockSpec((strands, verts), lambda i: (i, 0)),
        scratch_shapes=[pltpu.VMEM((screens * blocks, 2 * listed, verts), jnp.bfloat16)],
        compiler_params=pltpu.CompilerParams(vmem_limit_bytes=24 * 1024 * 1024),
    )(tiles, rows, data, tess_centre, tess_side)


def solution(mesh):
    return jax.shard_map(
        shards,
        mesh=mesh,
        in_specs=(
            P("scalp", None),
            P(("scalp", "screen"), None),
            P(("scalp", "screen"), None, None),
            P(("scalp", "screen"), None, None),
            P(("scalp", "screen"), None),
            P(("scalp", "screen"), None),
            P(("scalp", "screen"), None),
            P("screen", None, None),
            P("screen", None, None),
        ),
        out_specs=P(("scalp", "screen"), None),
        check_vma=False,
    )
```

```python
import functools

import jax
import jax.numpy as jnp
from jax import lax
from jax.experimental import pallas as pl
from jax.experimental.pallas import tpu as pltpu
from jax.sharding import PartitionSpec as P

MESH = pl.DeviceIdType.MESH
CHUNK = 1024


def columns(lists, lanes):
    parts = []
    for b in range(lists.shape[0]):
        row = jnp.broadcast_to(lists[b : b + 1, :], (lanes, lists.shape[1]))
        parts.append(row.T)
    return jnp.concatenate(parts, axis=0)


def pick_rows(wanted, guides, total):
    rows, lanes = wanted.shape
    tile = guides.shape[0]
    chunk = min(CHUNK, tile)
    lane = lax.broadcasted_iota(jnp.int32, (rows, lanes), 1)
    total[:rows] = jnp.zeros((rows, guides.shape[1]), jnp.float32)

    def body(i, carry):
        base = pl.multiple_of(i * chunk, chunk)
        hit = jnp.concatenate(
            [
                jnp.where(wanted == lane + (base + at), 1.0, 0.0).astype(jnp.bfloat16)
                for at in range(0, chunk, lanes)
            ],
            axis=1,
        )
        total[:rows] += jnp.dot(
            hit, guides[pl.ds(base, chunk), :], preferred_element_type=jnp.float32
        )
        return carry

    lax.fori_loop(0, tile // chunk, body, 0)
    return total[:rows].astype(jnp.bfloat16)


def exchange(
    scalps,
    guides_hbm,
    near_hbm,
    pick_hbm,
    weight,
    keep_hbm,
    width_hbm,
    route_hbm,
    centre_hbm,
    side_hbm,
    maps,
    spreads,
    tiles,
    guides,
    near,
    pick,
    keep,
    width,
    route,
    centre,
    side,
    rows,
    data,
    lists,
    outgoing,
    incoming,
    total,
    local_sem,
    send_sem,
    recv_sem,
):
    here = lax.axis_index("scalp")
    core = lax.axis_index("screen")
    lower = (lax.rem(here + scalps - 1, scalps), core)
    upper = (lax.rem(here + 1, scalps), core)
    pair = (here, 1 - core)
    tile = guides.shape[0]
    blocks, listed = near.shape
    joins, strands = pick.shape[1:]
    screens = data.shape[0]
    lanes = 128

    barrier = pltpu.get_barrier_semaphore()
    for other in (lower, upper, pair):
        pl.semaphore_signal(barrier, inc=1, device_id=other, device_id_type=MESH)
    loads = [
        pltpu.make_async_copy(src, dst, local_sem.at[at])
        for at, (src, dst) in enumerate(
            (
                (near_hbm, near),
                (pick_hbm, pick),
                (keep_hbm, keep),
                (width_hbm, width),
                (route_hbm, route),
                (guides_hbm, guides),
                (centre_hbm, centre),
                (side_hbm, side),
            )
        )
    ]
    for load in loads:
        load.start()

    def remote(src, dst, at, to):
        return pltpu.make_async_remote_copy(
            src_ref=src,
            dst_ref=dst,
            send_sem=send_sem.at[at],
            recv_sem=recv_sem.at[at],
            device_id=to,
            device_id_type=MESH,
        )

    loads[0].wait()
    pl.semaphore_wait(barrier, 3)
    ask_upper = remote(near, lists.at[0], 0, upper)
    ask_lower = remote(near, lists.at[1], 1, lower)
    ask_upper.start()
    ask_lower.start()

    for load in loads[1:5]:
        load.wait()
    kept = keep[...].astype(jnp.float32)
    scaled = width[...] * strands / (jnp.sum(kept, axis=1, keepdims=True) + 1.0)
    spare = data.shape[2] - 2 * joins - 2
    for b in range(blocks):
        data[core, b] = jnp.concatenate(
            [
                pick[b].astype(jnp.float32),
                weight[b].astype(jnp.float32),
                kept[b : b + 1],
                (kept * scaled)[b : b + 1],
                jnp.zeros((spare, strands), jnp.float32),
            ],
            axis=0,
        )
    tiles[core] = route[...]
    give_data = remote(data.at[core], data.at[core], 2, pair)
    give_data.start()
    give_tiles = remote(tiles.at[core], tiles.at[core], 3, pair)
    give_tiles.start()

    loads[5].wait()
    offset = here * tile
    ask_upper.wait()
    outgoing[0] = pick_rows(columns(lists[0], lanes) - offset, guides, total)
    to_lower = remote(outgoing.at[0], incoming.at[1], 4, lower)
    to_lower.start()
    ask_lower.wait()
    outgoing[1] = pick_rows(columns(lists[1], lanes) - offset, guides, total)
    to_upper = remote(outgoing.at[1], incoming.at[0], 5, upper)
    to_upper.start()

    rows[core] = pick_rows(columns(near[...], lanes) - offset, guides, total)
    give_data.wait()
    give_tiles.wait()
    names = lax.broadcasted_iota(jnp.int32, (listed, strands), 0).astype(jnp.float32)

    def mixing(at, carry):
        fields = data[at // blocks, at % blocks]
        mix = jnp.zeros((listed, strands), jnp.float32)
        for j in range(joins):
            mix = jnp.where(names == fields[j : j + 1], fields[joins + j : joins + j + 1], mix)
        spread = jnp.concatenate(
            [
                mix * fields[2 * joins : 2 * joins + 1],
                mix * fields[2 * joins + 1 : 2 * joins + 2],
            ],
            axis=0,
        )
        spreads[at] = spread.T.astype(jnp.bfloat16)
        return carry

    lax.fori_loop(0, screens * blocks, mixing, 0)
    loads[6].wait()
    loads[7].wait()
    to_lower.wait()
    to_upper.wait()
    rows[core] = rows[core] + incoming[0] + incoming[1]
    give_rows = remote(rows.at[core], rows.at[core], 6, pair)
    give_rows.start()

    def mapped(c):
        for half, table in enumerate((centre, side)):
            made = jnp.dot(rows[c], table[0], preferred_element_type=jnp.float32)
            made = made.astype(jnp.bfloat16)
            for b in range(blocks):
                maps[c, b, half * listed : (half + 1) * listed] = made[
                    b * listed : (b + 1) * listed
                ]

    mapped(core)
    give_rows.wait()
    mapped(1 - core)


def tessellate(cap, tiles, maps, spreads, out, held, sems):
    screens, blocks = maps.shape[:2]
    strands = spreads.shape[1]
    mine = lax.axis_index("screen")
    copies = []
    for source in range(screens):
        for place in range(cap):
            rank = jnp.int32(0)
            block = jnp.int32(0)
            found = jnp.int32(0)
            for b in range(blocks):
                same = (tiles[source, 0, b] == mine).astype(jnp.int32)
                hit = same * (rank == place).astype(jnp.int32)
                block = block + hit * b
                found = found + hit
                rank = rank + same
            slot = source * cap + place
            spread = spreads[source * blocks + block] * found.astype(jnp.float32).astype(
                jnp.bfloat16
            )
            held[slot] = jnp.dot(
                spread, maps[source, block], preferred_element_type=jnp.float32
            ).astype(out.dtype)
            copy = pltpu.make_async_copy(
                held.at[slot], out.at[pl.ds(slot * strands, strands)], sems.at[slot]
            )
            copy.start()
            copies.append(copy)
    for copy in copies:
        copy.wait()


def shards(guides, neighbours, pick, pick_weight, keep, width, route, tess_centre, tess_side):
    scalps = lax.axis_size("scalp")
    screens = lax.axis_size("screen")
    tile, points = guides.shape
    blocks, listed = neighbours.shape
    strands = keep.shape[1]
    joins = pick.shape[1]
    cap = blocks // screens + blocks // 4
    count = blocks * listed
    fields = -(-(2 * joins + 2) // 8) * 8
    verts = tess_centre.shape[2]
    vmem = pl.BlockSpec(memory_space=pltpu.VMEM)
    hbm = pl.BlockSpec(memory_space=pltpu.HBM)
    route = route.reshape(1, blocks)
    maps, spreads, tiles = pl.pallas_call(
        functools.partial(exchange, scalps),
        out_shape=(
            jax.ShapeDtypeStruct((screens, blocks, 2 * listed, verts), jnp.bfloat16),
            jax.ShapeDtypeStruct((screens * blocks, strands, 2 * listed), jnp.bfloat16),
            jax.ShapeDtypeStruct((screens, 1, blocks), jnp.int32),
        ),
        in_specs=[hbm, hbm, hbm, vmem, hbm, hbm, hbm, hbm, hbm],
        out_specs=(vmem, vmem, vmem),
        scratch_shapes=[
            pltpu.VMEM(guides.shape, guides.dtype),
            pltpu.VMEM(neighbours.shape, jnp.int32),
            pltpu.VMEM(pick.shape, jnp.int32),
            pltpu.VMEM(keep.shape, jnp.int32),
            pltpu.VMEM(width.shape, jnp.float32),
            pltpu.VMEM(route.shape, jnp.int32),
            pltpu.VMEM(tess_centre.shape, jnp.bfloat16),
            pltpu.VMEM(tess_side.shape, jnp.bfloat16),
            pltpu.VMEM((screens, count, points), jnp.bfloat16),
            pltpu.VMEM((screens, blocks, fields, strands), jnp.float32),
            pltpu.VMEM((2, blocks, listed), jnp.int32),
            pltpu.VMEM((2, count, points), jnp.bfloat16),
            pltpu.VMEM((2, count, points), jnp.bfloat16),
            pltpu.VMEM((count, points), jnp.float32),
            pltpu.SemaphoreType.DMA((8,)),
            pltpu.SemaphoreType.DMA((7,)),
            pltpu.SemaphoreType.DMA((7,)),
        ],
        compiler_params=pltpu.CompilerParams(
            collective_id=0, has_side_effects=True, vmem_limit_bytes=24 * 1024 * 1024
        ),
    )(guides, neighbours, pick, pick_weight, keep, width, route, tess_centre, tess_side)
    return pl.pallas_call(
        functools.partial(tessellate, cap),
        out_shape=jax.ShapeDtypeStruct((screens * cap * strands, verts), jnp.bfloat16),
        in_specs=[pl.BlockSpec(memory_space=pltpu.SMEM), vmem, vmem],
        out_specs=hbm,
        scratch_shapes=[
            pltpu.VMEM((screens * cap, strands, verts), jnp.bfloat16),
            pltpu.SemaphoreType.DMA((screens * cap,)),
        ],
        compiler_params=pltpu.CompilerParams(vmem_limit_bytes=24 * 1024 * 1024),
    )(tiles, maps, spreads)


def solution(mesh):
    return jax.shard_map(
        shards,
        mesh=mesh,
        in_specs=(
            P("scalp", None),
            P(("scalp", "screen"), None),
            P(("scalp", "screen"), None, None),
            P(("scalp", "screen"), None, None),
            P(("scalp", "screen"), None),
            P(("scalp", "screen"), None),
            P(("scalp", "screen"), None),
            P("screen", None, None),
            P("screen", None, None),
        ),
        out_specs=P(("scalp", "screen"), None),
        check_vma=False,
    )
```

```python
import functools

import jax
import jax.numpy as jnp
from jax import lax
from jax.experimental import pallas as pl
from jax.experimental.pallas import tpu as pltpu
from jax.sharding import PartitionSpec as P

MESH = pl.DeviceIdType.MESH
CHUNK = 1024


def columns(lists, lanes):
    parts = []
    for b in range(lists.shape[0]):
        row = jnp.broadcast_to(lists[b : b + 1, :], (lanes, lists.shape[1]))
        parts.append(row.T)
    return jnp.concatenate(parts, axis=0)


def pick_rows(wanted, guides, total):
    rows, lanes = wanted.shape
    tile = guides.shape[0]
    chunk = min(CHUNK, tile)
    lane = lax.broadcasted_iota(jnp.int32, (rows, lanes), 1)
    total[:rows] = jnp.zeros((rows, guides.shape[1]), jnp.float32)

    def body(i, carry):
        base = pl.multiple_of(i * chunk, chunk)
        hit = jnp.concatenate(
            [
                jnp.where(wanted == lane + (base + at), 1.0, 0.0).astype(jnp.bfloat16)
                for at in range(0, chunk, lanes)
            ],
            axis=1,
        )
        total[:rows] += jnp.dot(
            hit, guides[pl.ds(base, chunk), :], preferred_element_type=jnp.float32
        )
        return carry

    lax.fori_loop(0, tile // chunk, body, 0)
    return total[:rows].astype(jnp.bfloat16)


def exchange(
    scalps,
    guides_hbm,
    near_hbm,
    pick_hbm,
    weight,
    keep_hbm,
    width_hbm,
    route_hbm,
    centre_hbm,
    side_hbm,
    maps_hbm,
    spreads_hbm,
    tiles_hbm,
    maps,
    spreads,
    tiles,
    guides,
    near,
    pick,
    keep,
    width,
    route,
    centre,
    side,
    rows,
    data,
    lists,
    outgoing,
    incoming,
    total,
    local_sem,
    send_sem,
    recv_sem,
):
    here = lax.axis_index("scalp")
    core = lax.axis_index("screen")
    lower = (lax.rem(here + scalps - 1, scalps), core)
    upper = (lax.rem(here + 1, scalps), core)
    pair = (here, 1 - core)
    tile = guides.shape[0]
    blocks, listed = near.shape
    joins, strands = pick.shape[1:]
    screens = data.shape[0]
    lanes = 128

    barrier = pltpu.get_barrier_semaphore()
    for other in (lower, upper, pair):
        pl.semaphore_signal(barrier, inc=1, device_id=other, device_id_type=MESH)
    loads = [
        pltpu.make_async_copy(src, dst, local_sem.at[at])
        for at, (src, dst) in enumerate(
            (
                (near_hbm, near),
                (pick_hbm, pick),
                (keep_hbm, keep),
                (width_hbm, width),
                (route_hbm, route),
                (guides_hbm, guides),
                (centre_hbm, centre),
                (side_hbm, side),
            )
        )
    ]
    for load in loads:
        load.start()

    def remote(src, dst, at, to):
        return pltpu.make_async_remote_copy(
            src_ref=src,
            dst_ref=dst,
            send_sem=send_sem.at[at],
            recv_sem=recv_sem.at[at],
            device_id=to,
            device_id_type=MESH,
        )

    loads[0].wait()
    pl.semaphore_wait(barrier, 3)
    ask_upper = remote(near, lists.at[0], 0, upper)
    ask_lower = remote(near, lists.at[1], 1, lower)
    ask_upper.start()
    ask_lower.start()

    for load in loads[1:5]:
        load.wait()
    kept = keep[...].astype(jnp.float32)
    scaled = width[...] * strands / (jnp.sum(kept, axis=1, keepdims=True) + 1.0)
    spare = data.shape[2] - 2 * joins - 2
    for b in range(blocks):
        data[core, b] = jnp.concatenate(
            [
                pick[b].astype(jnp.float32),
                weight[b].astype(jnp.float32),
                kept[b : b + 1],
                (kept * scaled)[b : b + 1],
                jnp.zeros((spare, strands), jnp.float32),
            ],
            axis=0,
        )
    tiles[core] = route[...]
    give_data = remote(data.at[core], data.at[core], 2, pair)
    give_data.start()
    give_tiles = remote(tiles.at[core], tiles.at[core], 3, pair)
    give_tiles.start()

    loads[5].wait()
    offset = here * tile
    ask_upper.wait()
    outgoing[0] = pick_rows(columns(lists[0], lanes) - offset, guides, total)
    to_lower = remote(outgoing.at[0], incoming.at[1], 4, lower)
    to_lower.start()
    ask_lower.wait()
    outgoing[1] = pick_rows(columns(lists[1], lanes) - offset, guides, total)
    to_upper = remote(outgoing.at[1], incoming.at[0], 5, upper)
    to_upper.start()

    rows[core] = pick_rows(columns(near[...], lanes) - offset, guides, total)
    give_data.wait()
    give_tiles.wait()
    names = lax.broadcasted_iota(jnp.int32, (listed, strands), 0).astype(jnp.float32)

    def mixing(at, carry):
        fields = data[at // blocks, at % blocks]
        mix = jnp.zeros((listed, strands), jnp.float32)
        for j in range(joins):
            mix = jnp.where(names == fields[j : j + 1], fields[joins + j : joins + j + 1], mix)
        spread = jnp.concatenate(
            [
                mix * fields[2 * joins : 2 * joins + 1],
                mix * fields[2 * joins + 1 : 2 * joins + 2],
            ],
            axis=0,
        )
        spreads[at] = spread.T.astype(jnp.bfloat16)
        return carry

    lax.fori_loop(0, screens * blocks, mixing, 0)
    keep_tiles = pltpu.make_async_copy(tiles, tiles_hbm, local_sem.at[8])
    keep_tiles.start()
    keep_spreads = pltpu.make_async_copy(spreads, spreads_hbm, local_sem.at[9])
    keep_spreads.start()
    loads[6].wait()
    loads[7].wait()
    to_lower.wait()
    to_upper.wait()
    rows[core] = rows[core] + incoming[0] + incoming[1]
    give_rows = remote(rows.at[core], rows.at[core], 6, pair)
    give_rows.start()

    def mapped(c):
        for half, table in enumerate((centre, side)):
            made = jnp.dot(rows[c], table[0], preferred_element_type=jnp.float32)
            made = made.astype(jnp.bfloat16)
            for b in range(blocks):
                maps[c, b, half * listed : (half + 1) * listed] = made[
                    b * listed : (b + 1) * listed
                ]

    mapped(core)
    keep_own = pltpu.make_async_copy(maps.at[core], maps_hbm.at[core], local_sem.at[10])
    keep_own.start()
    give_rows.wait()
    mapped(1 - core)
    keep_other = pltpu.make_async_copy(
        maps.at[1 - core], maps_hbm.at[1 - core], local_sem.at[11]
    )
    keep_other.start()
    keep_tiles.wait()
    keep_spreads.wait()
    keep_own.wait()
    keep_other.wait()


def tessellate(
    cap, tiles_hbm, maps_hbm, spreads_hbm, out, tiles, maps, spreads, held, load_sems, sems
):
    screens, blocks = maps.shape[:2]
    strands = spreads.shape[1]
    mine = lax.axis_index("screen")
    load_tiles = pltpu.make_async_copy(tiles_hbm, tiles, load_sems.at[0])
    load_spreads = pltpu.make_async_copy(spreads_hbm, spreads, load_sems.at[1])
    load_maps = [
        pltpu.make_async_copy(maps_hbm.at[c], maps.at[c], load_sems.at[2 + c])
        for c in range(screens)
    ]
    for load in [load_tiles, load_spreads] + load_maps:
        load.start()
    load_tiles.wait()
    load_spreads.wait()
    copies = []
    for source in range(screens):
        load_maps[source].wait()
        for place in range(cap):
            rank = jnp.int32(0)
            block = jnp.int32(0)
            found = jnp.int32(0)
            for b in range(blocks):
                same = (tiles[source, 0, b] == mine).astype(jnp.int32)
                hit = same * (rank == place).astype(jnp.int32)
                block = block + hit * b
                found = found + hit
                rank = rank + same
            slot = source * cap + place
            spread = spreads[source * blocks + block] * found.astype(jnp.float32).astype(
                jnp.bfloat16
            )
            held[slot] = jnp.dot(
                spread, maps[source, block], preferred_element_type=jnp.float32
            ).astype(out.dtype)
            copy = pltpu.make_async_copy(
                held.at[slot], out.at[pl.ds(slot * strands, strands)], sems.at[slot]
            )
            copy.start()
            copies.append(copy)
    for copy in copies:
        copy.wait()


def shards(guides, neighbours, pick, pick_weight, keep, width, route, tess_centre, tess_side):
    scalps = lax.axis_size("scalp")
    screens = lax.axis_size("screen")
    tile, points = guides.shape
    blocks, listed = neighbours.shape
    strands = keep.shape[1]
    joins = pick.shape[1]
    cap = blocks // screens + blocks // 4
    count = blocks * listed
    fields = -(-(2 * joins + 2) // 8) * 8
    verts = tess_centre.shape[2]
    vmem = pl.BlockSpec(memory_space=pltpu.VMEM)
    hbm = pl.BlockSpec(memory_space=pltpu.HBM)
    route = route.reshape(1, blocks)
    maps, spreads, tiles = pl.pallas_call(
        functools.partial(exchange, scalps),
        out_shape=(
            jax.ShapeDtypeStruct((screens, blocks, 2 * listed, verts), jnp.bfloat16),
            jax.ShapeDtypeStruct((screens * blocks, strands, 2 * listed), jnp.bfloat16),
            jax.ShapeDtypeStruct((screens, 1, blocks), jnp.int32),
        ),
        in_specs=[hbm, hbm, hbm, vmem, hbm, hbm, hbm, hbm, hbm],
        out_specs=(hbm, hbm, hbm),
        scratch_shapes=[
            pltpu.VMEM((screens, blocks, 2 * listed, verts), jnp.bfloat16),
            pltpu.VMEM((screens * blocks, strands, 2 * listed), jnp.bfloat16),
            pltpu.VMEM((screens, 1, blocks), jnp.int32),
            pltpu.VMEM(guides.shape, guides.dtype),
            pltpu.VMEM(neighbours.shape, jnp.int32),
            pltpu.VMEM(pick.shape, jnp.int32),
            pltpu.VMEM(keep.shape, jnp.int32),
            pltpu.VMEM(width.shape, jnp.float32),
            pltpu.VMEM(route.shape, jnp.int32),
            pltpu.VMEM(tess_centre.shape, jnp.bfloat16),
            pltpu.VMEM(tess_side.shape, jnp.bfloat16),
            pltpu.VMEM((screens, count, points), jnp.bfloat16),
            pltpu.VMEM((screens, blocks, fields, strands), jnp.float32),
            pltpu.VMEM((2, blocks, listed), jnp.int32),
            pltpu.VMEM((2, count, points), jnp.bfloat16),
            pltpu.VMEM((2, count, points), jnp.bfloat16),
            pltpu.VMEM((count, points), jnp.float32),
            pltpu.SemaphoreType.DMA((12,)),
            pltpu.SemaphoreType.DMA((7,)),
            pltpu.SemaphoreType.DMA((7,)),
        ],
        compiler_params=pltpu.CompilerParams(
            collective_id=0, has_side_effects=True, vmem_limit_bytes=56 * 1024 * 1024
        ),
    )(guides, neighbours, pick, pick_weight, keep, width, route, tess_centre, tess_side)
    return pl.pallas_call(
        functools.partial(tessellate, cap),
        out_shape=jax.ShapeDtypeStruct((screens * cap * strands, verts), jnp.bfloat16),
        in_specs=[hbm, hbm, hbm],
        out_specs=hbm,
        scratch_shapes=[
            pltpu.SMEM((screens, 1, blocks), jnp.int32),
            pltpu.VMEM(maps.shape, jnp.bfloat16),
            pltpu.VMEM(spreads.shape, jnp.bfloat16),
            pltpu.VMEM((screens * cap, strands, verts), jnp.bfloat16),
            pltpu.SemaphoreType.DMA((2 + screens,)),
            pltpu.SemaphoreType.DMA((screens * cap,)),
        ],
        compiler_params=pltpu.CompilerParams(vmem_limit_bytes=56 * 1024 * 1024),
    )(tiles, maps, spreads)


def solution(mesh):
    return jax.shard_map(
        shards,
        mesh=mesh,
        in_specs=(
            P("scalp", None),
            P(("scalp", "screen"), None),
            P(("scalp", "screen"), None, None),
            P(("scalp", "screen"), None, None),
            P(("scalp", "screen"), None),
            P(("scalp", "screen"), None),
            P(("scalp", "screen"), None),
            P("screen", None, None),
            P("screen", None, None),
        ),
        out_specs=P(("scalp", "screen"), None),
        check_vma=False,
    )
```

```python
import functools

import jax
import jax.numpy as jnp
from jax import lax
from jax.experimental import pallas as pl
from jax.experimental.pallas import tpu as pltpu
from jax.sharding import PartitionSpec as P

MESH = pl.DeviceIdType.MESH
CHUNK = 1024


def columns(lists, lanes):
    parts = []
    for b in range(lists.shape[0]):
        row = jnp.broadcast_to(lists[b : b + 1, :], (lanes, lists.shape[1]))
        parts.append(row.T)
    return jnp.concatenate(parts, axis=0)


def pick_rows(wanted, guides, total):
    rows, lanes = wanted.shape
    tile = guides.shape[0]
    chunk = min(CHUNK, tile)
    lane = lax.broadcasted_iota(jnp.int32, (rows, lanes), 1)
    high = wanted >> (lanes.bit_length() - 1)
    low = jnp.where((wanted & (lanes - 1)) == lane, 1.0, 0.0).astype(jnp.bfloat16)
    total[:rows] = jnp.zeros((rows, guides.shape[1]), jnp.float32)

    def body(i, carry):
        base = pl.multiple_of(i * chunk, chunk)
        group = (high - i * (chunk // lanes)).astype(jnp.float32).astype(jnp.bfloat16)
        hit = jnp.concatenate(
            [
                jnp.where(group == jnp.bfloat16(at), low, jnp.bfloat16(0))
                for at in range(chunk // lanes)
            ],
            axis=1,
        )
        total[:rows] += jnp.dot(
            hit, guides[pl.ds(base, chunk), :], preferred_element_type=jnp.float32
        )
        return carry

    lax.fori_loop(0, tile // chunk, body, 0)
    return total[:rows].astype(jnp.bfloat16)


def exchange(
    scalps,
    guides_hbm,
    near_hbm,
    pick_hbm,
    weight_hbm,
    keep_hbm,
    width_hbm,
    route_hbm,
    centre_hbm,
    side_hbm,
    maps_hbm,
    spreads_hbm,
    tiles_hbm,
    maps,
    spreads,
    tiles,
    guides,
    near,
    pick,
    weight,
    keep,
    width,
    route,
    centre,
    side,
    rows,
    data,
    lists,
    outgoing,
    incoming,
    total,
    local_sem,
    send_sem,
    recv_sem,
):
    here = lax.axis_index("scalp")
    core = lax.axis_index("screen")
    lower = (lax.rem(here + scalps - 1, scalps), core)
    upper = (lax.rem(here + 1, scalps), core)
    pair = (here, 1 - core)
    tile = guides.shape[0]
    blocks, listed = near.shape
    joins, strands = pick.shape[1:]
    screens = data.shape[0]
    lanes = 128

    barrier = pltpu.get_barrier_semaphore()
    for other in (lower, upper, pair):
        pl.semaphore_signal(barrier, inc=1, device_id=other, device_id_type=MESH)
    loads = [
        pltpu.make_async_copy(src, dst, local_sem.at[at])
        for at, (src, dst) in enumerate(
            (
                (near_hbm, near),
                (pick_hbm, pick),
                (keep_hbm, keep),
                (width_hbm, width),
                (route_hbm, route),
                (guides_hbm, guides),
                (centre_hbm, centre),
                (side_hbm, side),
                (weight_hbm, weight),
            )
        )
    ]
    for load in loads:
        load.start()

    def remote(src, dst, at, to):
        return pltpu.make_async_remote_copy(
            src_ref=src,
            dst_ref=dst,
            send_sem=send_sem.at[at],
            recv_sem=recv_sem.at[at],
            device_id=to,
            device_id_type=MESH,
        )

    loads[0].wait()
    pl.semaphore_wait(barrier, 3)
    ask_upper = remote(near, lists.at[0], 0, upper)
    ask_lower = remote(near, lists.at[1], 1, lower)
    ask_upper.start()
    ask_lower.start()

    for load in loads[1:5] + loads[8:]:
        load.wait()
    kept = keep[...].astype(jnp.float32)
    scaled = width[...] * strands / (jnp.sum(kept, axis=1, keepdims=True) + 1.0)
    spare = data.shape[2] - 2 * joins - 2
    for b in range(blocks):
        data[core, b] = jnp.concatenate(
            [
                pick[b].astype(jnp.float32),
                weight[b].astype(jnp.float32),
                kept[b : b + 1],
                (kept * scaled)[b : b + 1],
                jnp.zeros((spare, strands), jnp.float32),
            ],
            axis=0,
        )
    tiles[core] = route[...]
    give_data = remote(data.at[core], data.at[core], 2, pair)
    give_data.start()
    give_tiles = remote(tiles.at[core], tiles.at[core], 3, pair)
    give_tiles.start()

    loads[5].wait()
    offset = here * tile
    ask_upper.wait()
    ask_lower.wait()
    wanted = jnp.concatenate([columns(lists[0], lanes), columns(lists[1], lanes)], axis=0)
    both = pick_rows(wanted - offset, guides, total)
    outgoing[0] = both[: blocks * listed]
    outgoing[1] = both[blocks * listed :]
    to_lower = remote(outgoing.at[0], incoming.at[1], 4, lower)
    to_lower.start()
    to_upper = remote(outgoing.at[1], incoming.at[0], 5, upper)
    to_upper.start()

    rows[core] = pick_rows(columns(near[...], lanes) - offset, guides, total)
    give_data.wait()
    give_tiles.wait()
    names = lax.broadcasted_iota(jnp.int32, (listed, strands), 0).astype(jnp.float32)

    def mixing(at, carry):
        fields = data[at // blocks, at % blocks]
        mix = jnp.zeros((listed, strands), jnp.float32)
        for j in range(joins):
            mix = jnp.where(names == fields[j : j + 1], fields[joins + j : joins + j + 1], mix)
        spread = jnp.concatenate(
            [
                mix * fields[2 * joins : 2 * joins + 1],
                mix * fields[2 * joins + 1 : 2 * joins + 2],
            ],
            axis=0,
        )
        spreads[at] = spread.T.astype(jnp.bfloat16)
        return carry

    lax.fori_loop(0, screens * blocks, mixing, 0)
    keep_tiles = pltpu.make_async_copy(tiles, tiles_hbm, local_sem.at[9])
    keep_tiles.start()
    keep_spreads = pltpu.make_async_copy(spreads, spreads_hbm, local_sem.at[10])
    keep_spreads.start()
    loads[6].wait()
    loads[7].wait()
    to_lower.wait()
    to_upper.wait()
    rows[core] = rows[core] + incoming[0] + incoming[1]
    give_rows = remote(rows.at[core], rows.at[core], 6, pair)
    give_rows.start()

    def mapped(c):
        for half, table in enumerate((centre, side)):
            made = jnp.dot(rows[c], table[0], preferred_element_type=jnp.float32)
            made = made.astype(jnp.bfloat16)
            for b in range(blocks):
                maps[c, b, half * listed : (half + 1) * listed] = made[
                    b * listed : (b + 1) * listed
                ]

    mapped(core)
    keep_own = pltpu.make_async_copy(maps.at[core], maps_hbm.at[core], local_sem.at[11])
    keep_own.start()
    give_rows.wait()
    mapped(1 - core)
    keep_other = pltpu.make_async_copy(
        maps.at[1 - core], maps_hbm.at[1 - core], local_sem.at[12]
    )
    keep_other.start()
    keep_tiles.wait()
    keep_spreads.wait()
    keep_own.wait()
    keep_other.wait()


def tessellate(
    cap, tiles_hbm, maps_hbm, spreads_hbm, out, tiles, maps, spreads, held, load_sems, sems
):
    screens, blocks = maps.shape[:2]
    strands = spreads.shape[1]
    mine = lax.axis_index("screen")
    load_tiles = pltpu.make_async_copy(tiles_hbm, tiles, load_sems.at[0])
    load_spreads = pltpu.make_async_copy(spreads_hbm, spreads, load_sems.at[1])
    load_maps = [
        pltpu.make_async_copy(maps_hbm.at[c], maps.at[c], load_sems.at[2 + c])
        for c in range(screens)
    ]
    for load in [load_tiles, load_spreads] + load_maps:
        load.start()
    load_tiles.wait()
    load_spreads.wait()
    copies = []
    for source in range(screens):
        load_maps[source].wait()
        for place in range(cap):
            rank = jnp.int32(0)
            block = jnp.int32(0)
            found = jnp.int32(0)
            for b in range(blocks):
                same = (tiles[source, 0, b] == mine).astype(jnp.int32)
                hit = same * (rank == place).astype(jnp.int32)
                block = block + hit * b
                found = found + hit
                rank = rank + same
            slot = source * cap + place
            spread = spreads[source * blocks + block] * found.astype(jnp.float32).astype(
                jnp.bfloat16
            )
            held[slot] = jnp.dot(
                spread, maps[source, block], preferred_element_type=jnp.float32
            ).astype(out.dtype)
            copy = pltpu.make_async_copy(
                held.at[slot], out.at[pl.ds(slot * strands, strands)], sems.at[slot]
            )
            copy.start()
            copies.append(copy)
    for copy in copies:
        copy.wait()


def shards(guides, neighbours, pick, pick_weight, keep, width, route, tess_centre, tess_side):
    scalps = lax.axis_size("scalp")
    screens = lax.axis_size("screen")
    tile, points = guides.shape
    blocks, listed = neighbours.shape
    strands = keep.shape[1]
    joins = pick.shape[1]
    cap = blocks // screens + blocks // 4
    count = blocks * listed
    fields = -(-(2 * joins + 2) // 8) * 8
    verts = tess_centre.shape[2]
    hbm = pl.BlockSpec(memory_space=pltpu.HBM)
    route = route.reshape(1, blocks)
    maps, spreads, tiles = pl.pallas_call(
        functools.partial(exchange, scalps),
        out_shape=(
            jax.ShapeDtypeStruct((screens, blocks, 2 * listed, verts), jnp.bfloat16),
            jax.ShapeDtypeStruct((screens * blocks, strands, 2 * listed), jnp.bfloat16),
            jax.ShapeDtypeStruct((screens, 1, blocks), jnp.int32),
        ),
        in_specs=[hbm, hbm, hbm, hbm, hbm, hbm, hbm, hbm, hbm],
        out_specs=(hbm, hbm, hbm),
        scratch_shapes=[
            pltpu.VMEM((screens, blocks, 2 * listed, verts), jnp.bfloat16),
            pltpu.VMEM((screens * blocks, strands, 2 * listed), jnp.bfloat16),
            pltpu.VMEM((screens, 1, blocks), jnp.int32),
            pltpu.VMEM(guides.shape, guides.dtype),
            pltpu.VMEM(neighbours.shape, jnp.int32),
            pltpu.VMEM(pick.shape, jnp.int32),
            pltpu.VMEM(pick_weight.shape, pick_weight.dtype),
            pltpu.VMEM(keep.shape, jnp.int32),
            pltpu.VMEM(width.shape, jnp.float32),
            pltpu.VMEM(route.shape, jnp.int32),
            pltpu.VMEM(tess_centre.shape, jnp.bfloat16),
            pltpu.VMEM(tess_side.shape, jnp.bfloat16),
            pltpu.VMEM((screens, count, points), jnp.bfloat16),
            pltpu.VMEM((screens, blocks, fields, strands), jnp.float32),
            pltpu.VMEM((2, blocks, listed), jnp.int32),
            pltpu.VMEM((2, count, points), jnp.bfloat16),
            pltpu.VMEM((2, count, points), jnp.bfloat16),
            pltpu.VMEM((2 * count, points), jnp.float32),
            pltpu.SemaphoreType.DMA((13,)),
            pltpu.SemaphoreType.DMA((7,)),
            pltpu.SemaphoreType.DMA((7,)),
        ],
        compiler_params=pltpu.CompilerParams(
            collective_id=0, has_side_effects=True, vmem_limit_bytes=56 * 1024 * 1024
        ),
    )(guides, neighbours, pick, pick_weight, keep, width, route, tess_centre, tess_side)
    return pl.pallas_call(
        functools.partial(tessellate, cap),
        out_shape=jax.ShapeDtypeStruct((screens * cap * strands, verts), jnp.bfloat16),
        in_specs=[hbm, hbm, hbm],
        out_specs=hbm,
        scratch_shapes=[
            pltpu.SMEM((screens, 1, blocks), jnp.int32),
            pltpu.VMEM(maps.shape, jnp.bfloat16),
            pltpu.VMEM(spreads.shape, jnp.bfloat16),
            pltpu.VMEM((screens * cap, strands, verts), jnp.bfloat16),
            pltpu.SemaphoreType.DMA((2 + screens,)),
            pltpu.SemaphoreType.DMA((screens * cap,)),
        ],
        compiler_params=pltpu.CompilerParams(vmem_limit_bytes=56 * 1024 * 1024),
    )(tiles, maps, spreads)


def solution(mesh):
    return jax.shard_map(
        shards,
        mesh=mesh,
        in_specs=(
            P("scalp", None),
            P(("scalp", "screen"), None),
            P(("scalp", "screen"), None, None),
            P(("scalp", "screen"), None, None),
            P(("scalp", "screen"), None),
            P(("scalp", "screen"), None),
            P(("scalp", "screen"), None),
            P("screen", None, None),
            P("screen", None, None),
        ),
        out_specs=P(("scalp", "screen"), None),
        check_vma=False,
    )
```

```python
import functools

import jax
import jax.numpy as jnp
from jax import lax
from jax.experimental import pallas as pl
from jax.experimental.pallas import tpu as pltpu
from jax.sharding import PartitionSpec as P

MESH = pl.DeviceIdType.MESH
CHUNK = 1024


def columns(lists, lanes):
    parts = []
    for b in range(lists.shape[0]):
        row = jnp.broadcast_to(lists[b : b + 1, :], (lanes, lists.shape[1]))
        parts.append(row.T)
    return jnp.concatenate(parts, axis=0)


def pick_rows(wanted, guides, total):
    rows, lanes = wanted.shape
    tile = guides.shape[0]
    chunk = min(CHUNK, tile)
    lane = lax.broadcasted_iota(jnp.int32, (rows, lanes), 1)
    high = wanted >> (lanes.bit_length() - 1)
    low = jnp.where((wanted & (lanes - 1)) == lane, 1.0, 0.0).astype(jnp.bfloat16)
    total[:rows] = jnp.zeros((rows, guides.shape[1]), jnp.float32)

    def body(i, carry):
        base = pl.multiple_of(i * chunk, chunk)
        group = (high - i * (chunk // lanes)).astype(jnp.float32).astype(jnp.bfloat16)
        hit = jnp.concatenate(
            [
                jnp.where(group == jnp.bfloat16(at), low, jnp.bfloat16(0))
                for at in range(chunk // lanes)
            ],
            axis=1,
        )
        total[:rows] += jnp.dot(
            hit, guides[pl.ds(base, chunk), :], preferred_element_type=jnp.float32
        )
        return carry

    lax.fori_loop(0, tile // chunk, body, 0)
    return total[:rows].astype(jnp.bfloat16)


def exchange(
    scalps,
    guides_hbm,
    near_hbm,
    pick_hbm,
    weight_hbm,
    keep_hbm,
    width_hbm,
    route_hbm,
    centre_hbm,
    side_hbm,
    maps_hbm,
    spreads_hbm,
    tiles_hbm,
    maps,
    spreads,
    tiles,
    guides,
    near,
    pick,
    weight,
    keep,
    width,
    route,
    centre,
    side,
    rows,
    data,
    lists,
    outgoing,
    incoming,
    total,
    local_sem,
    send_sem,
    recv_sem,
):
    here = lax.axis_index("scalp")
    core = lax.axis_index("screen")
    lower = (lax.rem(here + scalps - 1, scalps), core)
    upper = (lax.rem(here + 1, scalps), core)
    pair = (here, 1 - core)
    tile = guides.shape[0]
    blocks, listed = near.shape
    joins, strands = pick.shape[1:]
    screens = data.shape[0]
    lanes = 128

    barrier = pltpu.get_barrier_semaphore()
    for other in (lower, upper, pair):
        pl.semaphore_signal(barrier, inc=1, device_id=other, device_id_type=MESH)
    loads = [
        pltpu.make_async_copy(src, dst, local_sem.at[at])
        for at, (src, dst) in enumerate(
            (
                (near_hbm, near),
                (pick_hbm, pick),
                (keep_hbm, keep),
                (width_hbm, width),
                (route_hbm, route),
                (guides_hbm, guides),
                (centre_hbm, centre),
                (side_hbm, side),
                (weight_hbm, weight),
            )
        )
    ]
    for load in loads:
        load.start()

    def remote(src, dst, at, to):
        return pltpu.make_async_remote_copy(
            src_ref=src,
            dst_ref=dst,
            send_sem=send_sem.at[at],
            recv_sem=recv_sem.at[at],
            device_id=to,
            device_id_type=MESH,
        )

    loads[0].wait()
    pl.semaphore_wait(barrier, 3)
    ask_upper = remote(near, lists.at[0], 0, upper)
    ask_lower = remote(near, lists.at[1], 1, lower)
    ask_upper.start()
    ask_lower.start()

    for load in loads[1:5] + loads[8:]:
        load.wait()
    kept = keep[...].astype(jnp.float32)
    scaled = width[...] * strands / (jnp.sum(kept, axis=1, keepdims=True) + 1.0)
    spare = data.shape[2] - 2 * joins - 2
    for b in range(blocks):
        data[core, b] = jnp.concatenate(
            [
                pick[b].astype(jnp.float32),
                weight[b].astype(jnp.float32),
                kept[b : b + 1],
                (kept * scaled)[b : b + 1],
                jnp.zeros((spare, strands), jnp.float32),
            ],
            axis=0,
        )
    tiles[core] = route[...]
    give_data = remote(data.at[core], data.at[core], 2, pair)
    give_data.start()
    give_tiles = remote(tiles.at[core], tiles.at[core], 3, pair)
    give_tiles.start()

    loads[5].wait()
    offset = here * tile
    ask_upper.wait()
    ask_lower.wait()
    from_lower = columns(lists[0], lanes) - offset
    from_upper = columns(lists[1], lanes) - offset
    parts, part = rows.shape[1:3]
    to_lower, to_upper = [], []
    for h in range(parts):
        span = slice(h * part, (h + 1) * part)
        wanted = jnp.concatenate([from_lower[span], from_upper[span]], axis=0)
        both = pick_rows(wanted, guides, total)
        outgoing[0, h] = both[:part]
        outgoing[1, h] = both[part:]
        first = remote(outgoing.at[0, h], incoming.at[1, h], 4 + 2 * h, lower)
        first.start()
        to_lower.append(first)
        second = remote(outgoing.at[1, h], incoming.at[0, h], 5 + 2 * h, upper)
        second.start()
        to_upper.append(second)

    own = pick_rows(columns(near[...], lanes) - offset, guides, total)
    for h in range(parts):
        rows[core, h] = own[h * part : (h + 1) * part]
    give_data.wait()
    give_tiles.wait()
    names = lax.broadcasted_iota(jnp.int32, (listed, strands), 0).astype(jnp.float32)

    def mixing(at, carry):
        fields = data[at // blocks, at % blocks]
        mix = jnp.zeros((listed, strands), jnp.float32)
        for j in range(joins):
            mix = jnp.where(names == fields[j : j + 1], fields[joins + j : joins + j + 1], mix)
        spread = jnp.concatenate(
            [
                mix * fields[2 * joins : 2 * joins + 1],
                mix * fields[2 * joins + 1 : 2 * joins + 2],
            ],
            axis=0,
        )
        spreads[at] = spread.T.astype(jnp.bfloat16)
        return carry

    lax.fori_loop(0, screens * blocks, mixing, 0)
    keep_tiles = pltpu.make_async_copy(tiles, tiles_hbm, local_sem.at[9])
    keep_tiles.start()
    keep_spreads = pltpu.make_async_copy(spreads, spreads_hbm, local_sem.at[10])
    keep_spreads.start()
    loads[6].wait()
    loads[7].wait()

    group = blocks // parts
    keeps = []

    def mapped(c, h, at):
        for half, table in enumerate((centre, side)):
            made = jnp.dot(rows[c, h], table[0], preferred_element_type=jnp.float32)
            made = made.astype(jnp.bfloat16)
            for b in range(group):
                maps[c, h * group + b, half * listed : (half + 1) * listed] = made[
                    b * listed : (b + 1) * listed
                ]
        span = pl.ds(h * group, group)
        copy = pltpu.make_async_copy(maps.at[c, span], maps_hbm.at[c, span], local_sem.at[at])
        copy.start()
        keeps.append(copy)

    gives = []
    for h in range(parts):
        if h:
            mapped(core, h - 1, 9 + 2 + h - 1)
        to_lower[h].wait()
        to_upper[h].wait()
        rows[core, h] = rows[core, h] + incoming[0, h] + incoming[1, h]
        give = remote(rows.at[core, h], rows.at[core, h], 4 + 2 * parts + h, pair)
        give.start()
        gives.append(give)
    for h in range(parts):
        if h == parts - 1:
            mapped(core, h, 9 + 2 + h)
        gives[h].wait()
        mapped(1 - core, h, 9 + 2 + parts + h)
    keep_tiles.wait()
    keep_spreads.wait()
    for copy in keeps:
        copy.wait()


def tessellate(
    cap, tiles_hbm, maps_hbm, spreads_hbm, out, tiles, maps, spreads, held, load_sems, sems
):
    screens, blocks = maps.shape[:2]
    strands = spreads.shape[1]
    mine = lax.axis_index("screen")
    load_tiles = pltpu.make_async_copy(tiles_hbm, tiles, load_sems.at[0])
    load_spreads = pltpu.make_async_copy(spreads_hbm, spreads, load_sems.at[1])
    load_maps = [
        pltpu.make_async_copy(maps_hbm.at[c], maps.at[c], load_sems.at[2 + c])
        for c in range(screens)
    ]
    for load in [load_tiles, load_spreads] + load_maps:
        load.start()
    load_tiles.wait()
    load_spreads.wait()
    copies = []
    for source in range(screens):
        load_maps[source].wait()
        for place in range(cap):
            rank = jnp.int32(0)
            block = jnp.int32(0)
            found = jnp.int32(0)
            for b in range(blocks):
                same = (tiles[source, 0, b] == mine).astype(jnp.int32)
                hit = same * (rank == place).astype(jnp.int32)
                block = block + hit * b
                found = found + hit
                rank = rank + same
            slot = source * cap + place
            spread = spreads[source * blocks + block] * found.astype(jnp.float32).astype(
                jnp.bfloat16
            )
            held[slot] = jnp.dot(
                spread, maps[source, block], preferred_element_type=jnp.float32
            ).astype(out.dtype)
            copy = pltpu.make_async_copy(
                held.at[slot], out.at[pl.ds(slot * strands, strands)], sems.at[slot]
            )
            copy.start()
            copies.append(copy)
    for copy in copies:
        copy.wait()


def shards(guides, neighbours, pick, pick_weight, keep, width, route, tess_centre, tess_side):
    scalps = lax.axis_size("scalp")
    screens = lax.axis_size("screen")
    tile, points = guides.shape
    blocks, listed = neighbours.shape
    strands = keep.shape[1]
    joins = pick.shape[1]
    cap = blocks // screens + blocks // 4
    count = blocks * listed
    parts = 2 if blocks % 2 == 0 else 1
    part = count // parts
    fields = -(-(2 * joins + 2) // 8) * 8
    verts = tess_centre.shape[2]
    hbm = pl.BlockSpec(memory_space=pltpu.HBM)
    route = route.reshape(1, blocks)
    maps, spreads, tiles = pl.pallas_call(
        functools.partial(exchange, scalps),
        out_shape=(
            jax.ShapeDtypeStruct((screens, blocks, 2 * listed, verts), jnp.bfloat16),
            jax.ShapeDtypeStruct((screens * blocks, strands, 2 * listed), jnp.bfloat16),
            jax.ShapeDtypeStruct((screens, 1, blocks), jnp.int32),
        ),
        in_specs=[hbm, hbm, hbm, hbm, hbm, hbm, hbm, hbm, hbm],
        out_specs=(hbm, hbm, hbm),
        scratch_shapes=[
            pltpu.VMEM((screens, blocks, 2 * listed, verts), jnp.bfloat16),
            pltpu.VMEM((screens * blocks, strands, 2 * listed), jnp.bfloat16),
            pltpu.VMEM((screens, 1, blocks), jnp.int32),
            pltpu.VMEM(guides.shape, guides.dtype),
            pltpu.VMEM(neighbours.shape, jnp.int32),
            pltpu.VMEM(pick.shape, jnp.int32),
            pltpu.VMEM(pick_weight.shape, pick_weight.dtype),
            pltpu.VMEM(keep.shape, jnp.int32),
            pltpu.VMEM(width.shape, jnp.float32),
            pltpu.VMEM(route.shape, jnp.int32),
            pltpu.VMEM(tess_centre.shape, jnp.bfloat16),
            pltpu.VMEM(tess_side.shape, jnp.bfloat16),
            pltpu.VMEM((screens, parts, part, points), jnp.bfloat16),
            pltpu.VMEM((screens, blocks, fields, strands), jnp.float32),
            pltpu.VMEM((2, blocks, listed), jnp.int32),
            pltpu.VMEM((2, parts, part, points), jnp.bfloat16),
            pltpu.VMEM((2, parts, part, points), jnp.bfloat16),
            pltpu.VMEM((2 * count, points), jnp.float32),
            pltpu.SemaphoreType.DMA((11 + 2 * parts,)),
            pltpu.SemaphoreType.DMA((4 + 3 * parts,)),
            pltpu.SemaphoreType.DMA((4 + 3 * parts,)),
        ],
        compiler_params=pltpu.CompilerParams(
            collective_id=0, has_side_effects=True, vmem_limit_bytes=56 * 1024 * 1024
        ),
    )(guides, neighbours, pick, pick_weight, keep, width, route, tess_centre, tess_side)
    return pl.pallas_call(
        functools.partial(tessellate, cap),
        out_shape=jax.ShapeDtypeStruct((screens * cap * strands, verts), jnp.bfloat16),
        in_specs=[hbm, hbm, hbm],
        out_specs=hbm,
        scratch_shapes=[
            pltpu.SMEM((screens, 1, blocks), jnp.int32),
            pltpu.VMEM(maps.shape, jnp.bfloat16),
            pltpu.VMEM(spreads.shape, jnp.bfloat16),
            pltpu.VMEM((screens * cap, strands, verts), jnp.bfloat16),
            pltpu.SemaphoreType.DMA((2 + screens,)),
            pltpu.SemaphoreType.DMA((screens * cap,)),
        ],
        compiler_params=pltpu.CompilerParams(vmem_limit_bytes=56 * 1024 * 1024),
    )(tiles, maps, spreads)


def solution(mesh):
    return jax.shard_map(
        shards,
        mesh=mesh,
        in_specs=(
            P("scalp", None),
            P(("scalp", "screen"), None),
            P(("scalp", "screen"), None, None),
            P(("scalp", "screen"), None, None),
            P(("scalp", "screen"), None),
            P(("scalp", "screen"), None),
            P(("scalp", "screen"), None),
            P("screen", None, None),
            P("screen", None, None),
        ),
        out_specs=P(("scalp", "screen"), None),
        check_vma=False,
    )
```

```python
import functools

import jax
import jax.numpy as jnp
from jax import lax
from jax.experimental import pallas as pl
from jax.experimental.pallas import tpu as pltpu
from jax.sharding import PartitionSpec as P

MESH = pl.DeviceIdType.MESH
CHUNK = 1024


def columns(lists, lanes):
    parts = []
    for b in range(lists.shape[0]):
        row = jnp.broadcast_to(lists[b : b + 1, :], (lanes, lists.shape[1]))
        parts.append(row.T)
    return jnp.concatenate(parts, axis=0)


def pick_rows(wanted, guides, total):
    rows, lanes = wanted.shape
    tile = guides.shape[0]
    chunk = min(CHUNK, tile)
    lane = lax.broadcasted_iota(jnp.int32, (rows, lanes), 1)
    high = wanted >> (lanes.bit_length() - 1)
    low = jnp.where((wanted & (lanes - 1)) == lane, 1.0, 0.0).astype(jnp.bfloat16)
    total[:rows] = jnp.zeros((rows, guides.shape[1]), jnp.float32)

    def body(i, carry):
        base = pl.multiple_of(i * chunk, chunk)
        group = (high - i * (chunk // lanes)).astype(jnp.float32).astype(jnp.bfloat16)
        hit = jnp.concatenate(
            [
                jnp.where(group == jnp.bfloat16(at), low, jnp.bfloat16(0))
                for at in range(chunk // lanes)
            ],
            axis=1,
        )
        total[:rows] += jnp.dot(
            hit, guides[pl.ds(base, chunk), :], preferred_element_type=jnp.float32
        )
        return carry

    lax.fori_loop(0, tile // chunk, body, 0)
    return total[:rows].astype(jnp.bfloat16)


def exchange(
    scalps,
    cap,
    guides_hbm,
    near_hbm,
    pick_hbm,
    weight_hbm,
    keep_hbm,
    width_hbm,
    route_hbm,
    centre_hbm,
    side_hbm,
    out,
    tiles_smem,
    held,
    out_sems,
    maps,
    spreads,
    tiles,
    guides,
    near,
    pick,
    weight,
    keep,
    width,
    route,
    centre,
    side,
    rows,
    data,
    lists,
    outgoing,
    incoming,
    total,
    local_sem,
    send_sem,
    recv_sem,
):
    here = lax.axis_index("scalp")
    core = lax.axis_index("screen")
    lower = (lax.rem(here + scalps - 1, scalps), core)
    upper = (lax.rem(here + 1, scalps), core)
    pair = (here, 1 - core)
    tile = guides.shape[0]
    blocks, listed = near.shape
    joins, strands = pick.shape[1:]
    screens = data.shape[0]
    lanes = 128

    barrier = pltpu.get_barrier_semaphore()
    for other in (lower, upper, pair):
        pl.semaphore_signal(barrier, inc=1, device_id=other, device_id_type=MESH)
    loads = [
        pltpu.make_async_copy(src, dst, local_sem.at[at])
        for at, (src, dst) in enumerate(
            (
                (near_hbm, near),
                (pick_hbm, pick),
                (keep_hbm, keep),
                (width_hbm, width),
                (route_hbm, route),
                (guides_hbm, guides),
                (centre_hbm, centre),
                (side_hbm, side),
                (weight_hbm, weight),
            )
        )
    ]
    for load in loads:
        load.start()

    def remote(src, dst, at, to):
        return pltpu.make_async_remote_copy(
            src_ref=src,
            dst_ref=dst,
            send_sem=send_sem.at[at],
            recv_sem=recv_sem.at[at],
            device_id=to,
            device_id_type=MESH,
        )

    loads[0].wait()
    pl.semaphore_wait(barrier, 3)
    ask_upper = remote(near, lists.at[0], 0, upper)
    ask_lower = remote(near, lists.at[1], 1, lower)
    ask_upper.start()
    ask_lower.start()

    for load in loads[1:5] + loads[8:]:
        load.wait()
    kept = keep[...].astype(jnp.float32)
    scaled = width[...] * strands / (jnp.sum(kept, axis=1, keepdims=True) + 1.0)
    spare = data.shape[2] - 2 * joins - 2
    for b in range(blocks):
        data[core, b] = jnp.concatenate(
            [
                pick[b].astype(jnp.float32),
                weight[b].astype(jnp.float32),
                kept[b : b + 1],
                (kept * scaled)[b : b + 1],
                jnp.zeros((spare, strands), jnp.float32),
            ],
            axis=0,
        )
    tiles[core] = route[...]
    give_data = remote(data.at[core], data.at[core], 2, pair)
    give_data.start()
    give_tiles = remote(tiles.at[core], tiles.at[core], 3, pair)
    give_tiles.start()

    loads[5].wait()
    offset = here * tile
    ask_upper.wait()
    ask_lower.wait()
    wanted = jnp.concatenate([columns(lists[0], lanes), columns(lists[1], lanes)], axis=0)
    both = pick_rows(wanted - offset, guides, total)
    outgoing[0] = both[: blocks * listed]
    outgoing[1] = both[blocks * listed :]
    to_lower = remote(outgoing.at[0], incoming.at[1], 4, lower)
    to_lower.start()
    to_upper = remote(outgoing.at[1], incoming.at[0], 5, upper)
    to_upper.start()

    rows[core] = pick_rows(columns(near[...], lanes) - offset, guides, total)
    give_data.wait()
    give_tiles.wait()
    names = lax.broadcasted_iota(jnp.int32, (listed, strands), 0).astype(jnp.float32)

    def mixing(at, carry):
        fields = data[at // blocks, at % blocks]
        mix = jnp.zeros((listed, strands), jnp.float32)
        for j in range(joins):
            mix = jnp.where(names == fields[j : j + 1], fields[joins + j : joins + j + 1], mix)
        spread = jnp.concatenate(
            [
                mix * fields[2 * joins : 2 * joins + 1],
                mix * fields[2 * joins + 1 : 2 * joins + 2],
            ],
            axis=0,
        )
        spreads[at] = spread.T.astype(jnp.bfloat16)
        return carry

    lax.fori_loop(0, screens * blocks, mixing, 0)
    read_tiles = pltpu.make_async_copy(tiles, tiles_smem, local_sem.at[9])
    read_tiles.start()
    read_tiles.wait()
    loads[6].wait()
    loads[7].wait()
    to_lower.wait()
    to_upper.wait()
    rows[core] = rows[core] + incoming[0] + incoming[1]
    give_rows = remote(rows.at[core], rows.at[core], 6, pair)
    give_rows.start()

    def mapped(c):
        for half, table in enumerate((centre, side)):
            made = jnp.dot(rows[c], table[0], preferred_element_type=jnp.float32)
            made = made.astype(jnp.bfloat16)
            for b in range(blocks):
                maps[c, b, half * listed : (half + 1) * listed] = made[
                    b * listed : (b + 1) * listed
                ]

    copies = []
    for turn, source in enumerate((core, 1 - core)):
        if turn:
            give_rows.wait()
        mapped(source)
        for place in range(cap):
            rank = jnp.int32(0)
            block = jnp.int32(0)
            found = jnp.int32(0)
            for b in range(blocks):
                same = (tiles_smem[source, 0, b] == core).astype(jnp.int32)
                hit = same * (rank == place).astype(jnp.int32)
                block = block + hit * b
                found = found + hit
                rank = rank + same
            slot = source * cap + place
            spread = spreads[source * blocks + block] * found.astype(jnp.float32).astype(
                jnp.bfloat16
            )
            held[slot] = jnp.dot(
                spread, maps[source, block], preferred_element_type=jnp.float32
            ).astype(out.dtype)
            copy = pltpu.make_async_copy(
                held.at[slot],
                out.at[pl.ds(pl.multiple_of(slot * strands, strands), strands)],
                out_sems.at[turn * cap + place],
            )
            copy.start()
            copies.append(copy)
    for copy in copies:
        copy.wait()


def shards(guides, neighbours, pick, pick_weight, keep, width, route, tess_centre, tess_side):
    scalps = lax.axis_size("scalp")
    screens = lax.axis_size("screen")
    tile, points = guides.shape
    blocks, listed = neighbours.shape
    strands = keep.shape[1]
    joins = pick.shape[1]
    cap = blocks // screens + blocks // 4
    count = blocks * listed
    fields = -(-(2 * joins + 2) // 8) * 8
    verts = tess_centre.shape[2]
    hbm = pl.BlockSpec(memory_space=pltpu.HBM)
    route = route.reshape(1, blocks)
    return pl.pallas_call(
        functools.partial(exchange, scalps, cap),
        out_shape=jax.ShapeDtypeStruct((screens * cap * strands, verts), jnp.bfloat16),
        in_specs=[hbm, hbm, hbm, hbm, hbm, hbm, hbm, hbm, hbm],
        out_specs=hbm,
        scratch_shapes=[
            pltpu.SMEM((screens, 1, blocks), jnp.int32),
            pltpu.VMEM((screens * cap, strands, verts), jnp.bfloat16),
            pltpu.SemaphoreType.DMA((screens * cap,)),
            pltpu.VMEM((screens, blocks, 2 * listed, verts), jnp.bfloat16),
            pltpu.VMEM((screens * blocks, strands, 2 * listed), jnp.bfloat16),
            pltpu.VMEM((screens, 1, blocks), jnp.int32),
            pltpu.VMEM(guides.shape, guides.dtype),
            pltpu.VMEM(neighbours.shape, jnp.int32),
            pltpu.VMEM(pick.shape, jnp.int32),
            pltpu.VMEM(pick_weight.shape, pick_weight.dtype),
            pltpu.VMEM(keep.shape, jnp.int32),
            pltpu.VMEM(width.shape, jnp.float32),
            pltpu.VMEM(route.shape, jnp.int32),
            pltpu.VMEM(tess_centre.shape, jnp.bfloat16),
            pltpu.VMEM(tess_side.shape, jnp.bfloat16),
            pltpu.VMEM((screens, count, points), jnp.bfloat16),
            pltpu.VMEM((screens, blocks, fields, strands), jnp.float32),
            pltpu.VMEM((2, blocks, listed), jnp.int32),
            pltpu.VMEM((2, count, points), jnp.bfloat16),
            pltpu.VMEM((2, count, points), jnp.bfloat16),
            pltpu.VMEM((2 * count, points), jnp.float32),
            pltpu.SemaphoreType.DMA((10,)),
            pltpu.SemaphoreType.DMA((7,)),
            pltpu.SemaphoreType.DMA((7,)),
        ],
        compiler_params=pltpu.CompilerParams(
            collective_id=0, has_side_effects=True, vmem_limit_bytes=56 * 1024 * 1024
        ),
    )(guides, neighbours, pick, pick_weight, keep, width, route, tess_centre, tess_side)


def solution(mesh):
    return jax.shard_map(
        shards,
        mesh=mesh,
        in_specs=(
            P("scalp", None),
            P(("scalp", "screen"), None),
            P(("scalp", "screen"), None, None),
            P(("scalp", "screen"), None, None),
            P(("scalp", "screen"), None),
            P(("scalp", "screen"), None),
            P(("scalp", "screen"), None),
            P("screen", None, None),
            P("screen", None, None),
        ),
        out_specs=P(("scalp", "screen"), None),
        check_vma=False,
    )
```
